1024 devices in a mesh: gx: 32 (over x_lo, z), gy: 8 (over y), dev: 4 (over x_hi, core).
Axes of the slice: x: 4 (x_hi: 2, x_lo: 2; x = x_hi * 2 + x_lo), y: 8, z: 16, core: 2. Of those that a mesh axis runs over, the one named last changes fastest.
Arguments:
- activations: bfloat16 [9216, 512], P(('gy', 'gx'), 'dev'), may hold values from -6 to 6
- weight_in: bfloat16 [9216, 36864], P('gy', 'gx'), may hold values from -0.125 to 0.125
- weight_out: bfloat16 [36864, 9216], P('gx', 'gy'), may hold values from -0.0625 to 0.0625
- cotangent: bfloat16 [9216, 512], P(('gy', 'gx'), 'dev'), may hold values from -6 to 6
Outputs:
- outputs: bfloat16 [9216, 512], P(('gy', 'gx'), 'dev')
- grad_inputs: bfloat16 [9216, 512], P(('gy', 'gx'), 'dev')
- grad_weight_in: bfloat16 [9216, 36864], P(('gy', 'dev'), 'gx')
- grad_weight_out: bfloat16 [36864, 9216], P(('gx', 'dev'), 'gy')
The draws below stay inside these ranges and needn't reach their ends.
All inputs are finite; a program needn't handle non-finite values.
Results may differ from the reference program's by a relative error of at most 0.0049.
Values may be sent and summed in bfloat16 or wider, within the bound.
No kernel may reach another device: no remote copies, remote signals or barrier semaphores. Data moves between devices by JAX's collectives and lax.ppermute only.
A program may use at most 32 MiB of HBM per device.

```python
import math
import jax
import jax.numpy as jnp
from jax import lax

D = 9216
FF = 36864
TOKENS = 512


def with_spikes(entries, stream_key, source, target, shards_of, factor):
    owner, partner = [(jnp.arange(entries.shape[axis_at]) // (entries.shape[axis_at] // shards_of)).reshape([-1 if axis == axis_at else 1 for axis in range(entries.ndim)]) for axis_at in (source, target)]
    chosen = jax.random.permutation(stream_key, shards_of)[partner]
    strong = (owner == chosen) | (owner == (partner + shards_of // 2) % shards_of)
    return jnp.where(strong, factor * entries, entries)


def levels(own_key, shape, pieces, low, top_value):
    level = 1.0
    for dim, parts in pieces:
        heights = jax.random.uniform(jax.random.fold_in(jax.random.fold_in(own_key, 6), dim), (parts,), jnp.float32, low / len(pieces), top_value / len(pieces))
        level = level * jnp.repeat(jnp.exp(heights), shape[dim] // parts).reshape((-1,) + (1,) * (len(shape) - 1 - dim))
    return level


def gaussian(rng, extent, scale, limit, cuts=(), held_as=jnp.bfloat16):
    factor_of = levels(rng, extent, cuts, -0.22, 0.18) if cuts else 1.0
    array = jax.random.normal(rng, extent, jnp.float32) * scale * factor_of
    return jnp.minimum(jnp.maximum(array, -limit), limit).astype(held_as)


def gaussian_with(rng, extent, deviation, limit, pieces, heavy, kind=jnp.bfloat16):
    values = deviation * jax.random.normal(rng, extent, jnp.float32)
    if pieces:
        values = values * levels(rng, extent, pieces, -0.22, 0.18)
    return jnp.clip(with_spikes(values, jax.random.fold_in(rng, 3), *heavy), -limit, limit).astype(kind)


def setup_inputs(seed: int = 0) -> dict:
    splits = jax.random.split(jax.random.key(seed), 5)
    return {
        "activations": gaussian(splits[0], (D, TOKENS), 1.0, 6.0, ((0, 256), (1, 4))),
        "weight_in": gaussian_with(splits[1], (D, FF), D ** -0.5, 0.125, ((0, 8), (1, 32)), (1, 0, 32, 2.75)),
        "weight_out": gaussian_with(splits[2], (FF, D), FF ** -0.5, 0.0625, ((0, 32), (1, 8)), (0, 1, 32, 2.75)),
        "cotangent": gaussian(splits[3], (D, TOKENS), 1.0, 6.0, ((0, 256), (1, 4))),
    }


def silu_slope(pre):
    sig = jax.nn.sigmoid(pre)
    return sig * (1.0 + pre * (1.0 - sig))

def contract_first(left, right):
    return lax.dot_general(left, right, (((0,), (0,)), ((), ())), preferred_element_type=jnp.float32)

def contract_last(left, right):
    return lax.dot_general(left, right, (((1,), (1,)), ((), ())), preferred_element_type=jnp.float32)

def reference(activations, weight_in, weight_out, cotangent):
    factor = 1.0 / math.sqrt(activations.shape[1])
    pre = contract_first(weight_in, activations)
    hidden = jax.nn.silu(pre).astype(jnp.bfloat16)
    outputs = contract_first(weight_out, hidden).astype(jnp.bfloat16)
    grad_hidden = jnp.dot(weight_out, cotangent, preferred_element_type=jnp.float32)
    grad_pre = (grad_hidden * silu_slope(pre)).astype(jnp.bfloat16)
    grad_inputs = jnp.dot(weight_in, grad_pre, preferred_element_type=jnp.float32).astype(jnp.bfloat16)
    grad_weight_in = (contract_last(activations, grad_pre) * factor).astype(jnp.bfloat16)
    grad_weight_out = (contract_last(hidden, cotangent) * factor).astype(jnp.bfloat16)
    return (outputs, grad_inputs, grad_weight_in, grad_weight_out)
```

```python
import math

import jax
import jax.numpy as jnp
from jax import lax
from jax.sharding import Mesh, PartitionSpec as P

F32 = jnp.float32
BF16 = jnp.bfloat16


def silu_slope(pre):
    sig = jax.nn.sigmoid(pre)
    return sig * (1.0 + pre * (1.0 - sig))


def dot(left, right, contract):
    return lax.dot_general(left, right, (contract, ((), ())), preferred_element_type=F32)


def body(activations, weight_in, weight_out, cotangent):
    own, tokens = activations.shape
    feats, units = weight_in.shape
    n_gx = lax.axis_size("xl") * lax.axis_size("z")
    n_gy = lax.axis_size("gy")
    n_dev = lax.axis_size("xh") * lax.axis_size("core")
    share = units // n_gy

    pair = jnp.concatenate([activations, cotangent], axis=0)
    block = lax.all_gather(pair, "z", axis=0, tiled=False)
    block = lax.all_gather(block, "xl", axis=0, tiled=True)
    acts = block[:, :own].reshape(feats, tokens)
    cots = block[:, own:].reshape(feats, tokens)
    block_all = lax.all_gather(block, ("xh", "core"), axis=0, tiled=False)

    pre_part = dot(weight_in, acts, ((0,), (0,))).astype(BF16).reshape(n_gy, share, tokens)
    grad_part = dot(weight_out, cots, ((1,), (0,))).astype(BF16).reshape(n_gy, share, tokens)
    parts = lax.all_to_all(
        jnp.concatenate([pre_part, grad_part], axis=1), "gy", 0, 0, tiled=True
    )
    total = jnp.sum(parts.astype(F32), axis=0)
    pre, grad_hidden = total[:share], total[share:]
    hidden = jax.nn.silu(pre).astype(BF16)
    grad_pre = (grad_hidden * silu_slope(pre)).astype(BF16)
    both = lax.all_gather(jnp.concatenate([hidden, grad_pre], axis=0), "gy", axis=0, tiled=False)
    both_all = lax.all_gather(both, ("xh", "core"), axis=0, tiled=False)
    hidden_block = both[:, :share].reshape(units, tokens)
    grad_block = both[:, share:].reshape(units, tokens)

    out_part = dot(weight_out, hidden_block, ((0,), (0,))).astype(BF16).reshape(n_gx, own, tokens)
    in_part = dot(weight_in, grad_block, ((1,), (0,))).astype(BF16).reshape(n_gx, own, tokens)
    sums = lax.all_to_all(
        jnp.concatenate([out_part, in_part], axis=1), ("xl", "z"), 0, 0, tiled=True
    )
    sums = jnp.sum(sums.astype(F32), axis=0).astype(BF16)
    outputs, grad_inputs = sums[:own], sums[own:]

    owner = lax.axis_index("xh") * lax.axis_size("core") + lax.axis_index("core")
    rows = n_gx // n_dev
    acts_own = lax.dynamic_slice_in_dim(block_all, owner * rows, rows, 1)[:, :, :own]
    acts_own = acts_own.reshape(n_dev, rows * own, tokens)
    cots_all = block_all[:, :, own:].reshape(n_dev, feats, tokens)
    chunks = n_gy // n_dev
    hidden_own = lax.dynamic_slice_in_dim(both_all, owner * chunks, chunks, 1)[:, :, :share]
    hidden_own = hidden_own.reshape(n_dev, chunks * share, tokens)
    grads_all = both_all[:, :, share:].reshape(n_dev, units, tokens)
    factor = 1.0 / math.sqrt(n_dev * tokens)
    grad_weight_in = dot(acts_own, grads_all, ((0, 2), (0, 2)))
    grad_weight_out = dot(hidden_own, cots_all, ((0, 2), (0, 2)))
    return (
        outputs,
        grad_inputs,
        (grad_weight_in * factor).astype(BF16),
        (grad_weight_out * factor).astype(BF16),
    )


def solution(mesh):
    shape = mesh.devices.shape
    fine = Mesh(
        mesh.devices.reshape(2, shape[0] // 2, shape[1], 2, shape[2] // 2),
        ("xl", "z", "gy", "xh", "core"),
    )
    gx, dev = ("xl", "z"), ("xh", "core")
    return jax.shard_map(
        body,
        mesh=fine,
        in_specs=(P(("gy", *gx), dev), P("gy", gx), P(gx, "gy"), P(("gy", *gx), dev)),
        out_specs=(P(("gy", *gx), dev), P(("gy", *gx), dev), P(("gy", *dev), gx), P((*gx, *dev), "gy")),
        check_vma=False,
    )
```

```python
import functools
import math

import jax
import jax.numpy as jnp
from jax import lax
from jax.experimental import pallas as pl
from jax.experimental.pallas import tpu as pltpu
from jax.sharding import Mesh, PartitionSpec as P

F32 = jnp.float32
BF16 = jnp.bfloat16
GX = ("xl", "z")
DEV = ("xh", "core")
VMEM = pl.BlockSpec(memory_space=pltpu.VMEM)


def silu_slope(pre):
    sig = jax.nn.sigmoid(pre)
    return sig * (1.0 + pre * (1.0 - sig))


def dot(left, right, contract):
    return lax.dot_general(left, right, (contract, ((), ())), preferred_element_type=F32)


def turned(right):
    return right.astype(F32).T.astype(BF16)


class Weights:
    def __init__(self, rows_hbm, columns_hbm, rows_ref, columns_ref, sems):
        self.rows_ref, self.columns_ref = rows_ref, columns_ref
        self.width = rows_ref.shape[0] // sems.shape[1]
        self.parts = [pl.ds(c * self.width, self.width) for c in range(sems.shape[1])]
        self.rows = [
            pltpu.make_async_copy(rows_hbm.at[part], rows_ref.at[part], sems.at[0, c])
            for c, part in enumerate(self.parts)
        ]
        self.columns = [
            pltpu.make_async_copy(columns_hbm.at[:, part], columns_ref.at[:, part], sems.at[1, c])
            for c, part in enumerate(self.parts)
        ]
        for copy in self.rows + self.columns:
            copy.start()

    def rows_dot(self, right, to_ref):
        for part, copy in zip(self.parts, self.rows):
            copy.wait()
            to_ref[part] = dot(self.rows_ref[part], right, ((1,), (0,)))

    def columns_dot(self, left, to_ref):
        for part, copy in zip(self.parts, self.columns):
            copy.wait()
            to_ref[part] = dot(left, self.columns_ref[:, part], ((1,), (0,))).T


def unit_terms(block_ref, in_hbm, out_hbm, parts_ref, out_ref, in_ref, acts_ref, cots_ref, pair_ref, sems):
    weights = Weights(out_hbm, in_hbm, out_ref, in_ref, sems)
    own = block_ref.shape[1] // 2
    for g in range(block_ref.shape[0]):
        pair_ref[...] = block_ref[g].astype(F32)
        acts_ref[g * own : (g + 1) * own] = pair_ref[:own]
        cots_ref[g * own : (g + 1) * own] = pair_ref[own:]
    cots, acts = cots_ref[...].astype(BF16), turned(acts_ref[...])
    grad_ref, pre_ref = cots_ref, acts_ref
    weights.rows_dot(cots, grad_ref)
    weights.columns_dot(acts, pre_ref)
    share = parts_ref.shape[1] // 2
    for k in range(parts_ref.shape[0]):
        at = pl.ds(k * share, share)
        parts_ref[k, :share] = pre_ref[at].astype(BF16)
        parts_ref[k, share:] = grad_ref[at].astype(BF16)


def feature_terms(both_ref, in_hbm, out_hbm, sums_ref, in_ref, out_ref, out_rows_ref, in_rows_ref, pair_ref, sems):
    weights = Weights(in_hbm, out_hbm, in_ref, out_ref, sems)
    share = both_ref.shape[1] // 2
    shares = range(both_ref.shape[0])
    hidden = turned(jnp.concatenate([both_ref[k, :share] for k in shares], axis=0))
    grad = jnp.concatenate([both_ref[k, share:] for k in shares], axis=0)
    weights.rows_dot(grad, in_rows_ref)
    weights.columns_dot(hidden, out_rows_ref)
    own = sums_ref.shape[1] // 2
    for g in range(sums_ref.shape[0]):
        pair_ref[:own] = out_rows_ref[g * own : (g + 1) * own]
        pair_ref[own:] = in_rows_ref[g * own : (g + 1) * own]
        sums_ref[g] = pair_ref[...].astype(BF16)


def unpack(block_hbm, acts_out, cots_out, block_ref, acts_ref, cots_ref, pair_ref, sems):
    groups, members, rows, tokens = block_ref.shape
    own = rows // 2
    copies = [
        pltpu.make_async_copy(block_hbm.at[t], block_ref.at[t], sems.at[t]) for t in range(groups)
    ]
    for copy in copies:
        copy.start()
    owner = lax.axis_index(DEV)
    for t in range(groups):
        copies[t].wait()
        lanes = slice(t * tokens, (t + 1) * tokens)
        for g in range(members):
            pair_ref[...] = block_ref[t, g].astype(F32)
            cots_ref[g * own : (g + 1) * own] = pair_ref[own:]
        cots_out[:, lanes] = cots_ref[...].astype(BF16)
        for g in range(members // groups):
            pair_ref[...] = block_ref[t, owner * (members // groups) + g].astype(F32)
            acts_ref[g * own : (g + 1) * own] = pair_ref[:own]
        acts_out[:, lanes] = acts_ref[...].astype(BF16)


def weight_grads(factor, acts_ref, cots_ref, both_hbm, in_ref, out_ref, grads_ref, hidden_ref, sems):
    groups, _, share, _ = grads_ref.shape
    pieces = hidden_ref.shape[1]
    shares = grads_ref.shape[1]
    first = lax.axis_index(DEV) * pieces
    copies = [
        pltpu.make_async_copy(
            both_hbm.at[:, pl.ds(k, 2), pl.ds(share, share)], grads_ref.at[:, pl.ds(k, 2)], sems.at[k // 2]
        )
        for k in range(0, shares, 2)
    ]
    copies.append(
        pltpu.make_async_copy(
            both_hbm.at[:, pl.ds(first, pieces), pl.ds(0, share)], hidden_ref, sems.at[shares // 2]
        )
    )
    for copy in copies:
        copy.start()

    def beside(ref, at, count):
        return jnp.concatenate(
            [
                jnp.concatenate([ref[t, at + j] for j in range(count)], axis=0)
                for t in range(groups)
            ],
            axis=1,
        )

    acts = acts_ref[...]
    for k in (0, 2, 4, 6):
        copies[k // 2].wait()
    width = 384
    every = beside(grads_ref, 0, shares)
    for at in range(0, in_ref.shape[1], width):
        part = every[at : at + width]
        in_ref[:, at : at + width] = (dot(acts, part, ((1,), (1,))) * factor).astype(BF16)
    copies[-1].wait()
    hidden = beside(hidden_ref, 0, pieces)
    for at in range(0, out_ref.shape[1], width):
        part = cots_ref[at : at + width]
        out_ref[:, at : at + width] = (dot(hidden, part, ((1,), (1,))) * factor).astype(BF16)


def call(kernel, name, outs, scratch, n_sems, args, in_hbm, flops, vmem):
    n_bytes = sum(a.size * a.dtype.itemsize for a in args)
    return pl.pallas_call(
        kernel,
        out_shape=outs,
        in_specs=[pl.BlockSpec(memory_space=pltpu.HBM) if i in in_hbm else VMEM for i in range(len(args))],
        out_specs=jax.tree.map(lambda _: VMEM, outs),
        scratch_shapes=[pltpu.VMEM(*s) for s in scratch] + [pltpu.SemaphoreType.DMA(n_sems)],
        compiler_params=pltpu.CompilerParams(vmem_limit_bytes=vmem * 2**20),
        cost_estimate=pl.CostEstimate(flops=flops, bytes_accessed=n_bytes, transcendentals=0),
        name=name,
    )(*args)


def spread(local, axes):
    copies = jnp.broadcast_to(local[None], (lax.axis_size(axes), *local.shape))
    return lax.all_to_all(copies, axes, 0, 0, tiled=True)


def body(activations, weight_in, weight_out, cotangent):
    own, tokens = activations.shape
    feats, units = weight_in.shape
    n_gx, n_gy, n_dev = (lax.axis_size(a) for a in (GX, "gy", DEV))
    share = units // n_gy
    pair_rows = (2 * own, tokens)
    products = 4 * feats * units * tokens

    pair = jnp.concatenate([activations, cotangent], axis=0)
    block = lax.all_gather(pair, "z", axis=0, tiled=False)
    block = lax.all_gather(block, "xl", axis=0, tiled=True)
    block_all = lax.all_gather(block, DEV, axis=0, tiled=False)

    weight = (weight_in.shape, BF16)
    rows = ((feats, tokens), F32)
    parts = call(
        unit_terms,
        "unit_terms",
        jax.ShapeDtypeStruct((n_gy, 2 * share, tokens), BF16),
        [weight, weight, rows, rows, (pair_rows, F32)],
        (2, 3),
        (block, weight_in, weight_out),
        (1, 2),
        products,
        62,
    )
    parts = lax.all_to_all(parts, "gy", 0, 0, tiled=True)
    total = jnp.sum(parts.astype(F32), axis=0)
    pre, grad_hidden = total[:share], total[share:]
    hidden = jax.nn.silu(pre).astype(BF16)
    grad_pre = (grad_hidden * silu_slope(pre)).astype(BF16)
    both = spread(jnp.concatenate([hidden, grad_pre], axis=0), "gy").reshape(n_gy, 2 * share, tokens)
    both_all = lax.all_gather(both, DEV, axis=0, tiled=False)

    sums = call(
        feature_terms,
        "feature_terms",
        jax.ShapeDtypeStruct((n_gx, *pair_rows), BF16),
        [weight, weight, rows, rows, (pair_rows, F32)],
        (2, 3),
        (both, weight_in, weight_out),
        (1, 2),
        products,
        62,
    )
    sums = lax.all_to_all(sums, GX, 0, 0, tiled=True)
    sums = jnp.sum(sums.astype(F32), axis=0).astype(BF16)

    acts_own, cots_all = call(
        unpack,
        "unpack",
        (
            jax.ShapeDtypeStruct((feats // n_dev, n_dev * tokens), BF16),
            jax.ShapeDtypeStruct((feats, n_dev * tokens), BF16),
        ),
        [
            (block_all.shape, BF16),
            ((feats // n_dev, tokens), F32),
            ((feats, tokens), F32),
            (pair_rows, F32),
        ],
        (n_dev,),
        (block_all,),
        (0,),
        products,
        62,
    )
    grads = call(
        functools.partial(weight_grads, 1.0 / math.sqrt(n_dev * tokens)),
        "weight_grads",
        (
            jax.ShapeDtypeStruct((feats // n_dev, units), BF16),
            jax.ShapeDtypeStruct((units // n_dev, feats), BF16),
        ),
        [
            ((n_dev, n_gy, share, tokens), BF16),
            ((n_dev, n_gy // n_dev, share, tokens), BF16),
        ],
        (n_gy // 2 + 1,),
        (acts_own, cots_all, both_all),
        (2,),
        products,
        60,
    )
    return (sums[:own], sums[own:], *grads)


def solution(mesh):
    shape = mesh.devices.shape
    fine = Mesh(
        mesh.devices.reshape(2, shape[0] // 2, shape[1], 2, shape[2] // 2),
        ("xl", "z", "gy", "xh", "core"),
    )
    return jax.shard_map(
        body,
        mesh=fine,
        in_specs=(P(("gy", *GX), DEV), P("gy", GX), P(GX, "gy"), P(("gy", *GX), DEV)),
        out_specs=(P(("gy", *GX), DEV), P(("gy", *GX), DEV), P(("gy", *DEV), GX), P((*GX, *DEV), "gy")),
        check_vma=False,
    )
```

```python
import functools
import math

import jax
import jax.numpy as jnp
from jax import lax
from jax.experimental import pallas as pl
from jax.experimental.pallas import tpu as pltpu
from jax.sharding import Mesh, PartitionSpec as P

F32 = jnp.float32
BF16 = jnp.bfloat16
GX = ("xl", "z")
DEV = ("xh", "core")
VMEM = pl.BlockSpec(memory_space=pltpu.VMEM)


def silu_slope(pre):
    sig = jax.nn.sigmoid(pre)
    return sig * (1.0 + pre * (1.0 - sig))


def dot(left, right, contract):
    return lax.dot_general(left, right, (contract, ((), ())), preferred_element_type=F32)


def turned(right):
    return right.astype(F32).T.astype(BF16)


class Weights:
    def __init__(self, columns_hbm, rows_hbm, columns_ref, rows_ref, sems):
        n = sems.shape[1]
        self.columns_ref, self.rows_ref = columns_ref, rows_ref
        self.column_parts = [pl.ds(c * (columns_ref.shape[1] // 3), columns_ref.shape[1] // 3) for c in range(3)]
        self.row_parts = [pl.ds(c * (rows_ref.shape[0] // n), rows_ref.shape[0] // n) for c in range(n)]
        self.columns = [
            pltpu.make_async_copy(columns_hbm.at[:, part], columns_ref.at[:, part], sems.at[0, c])
            for c, part in enumerate(self.column_parts)
        ]
        self.rows = [
            pltpu.make_async_copy(rows_hbm.at[part], rows_ref.at[part], sems.at[1, c])
            for c, part in enumerate(self.row_parts)
        ]
        for copy in self.columns + self.rows:
            copy.start()

    def columns_dot(self, left, to_ref):
        for part, copy in zip(self.column_parts, self.columns):
            copy.wait()
            to_ref[part] = dot(left, self.columns_ref[:, part], ((1,), (0,))).T

    def rows_dot(self, right):
        for part, copy in zip(self.row_parts, self.rows):
            copy.wait()
            yield dot(self.rows_ref[part], right, ((1,), (0,)))


def unit_terms(block_ref, in_hbm, out_hbm, parts_ref, in_ref, out_ref, acts_ref, cots_ref, pair_ref, sems):
    weights = Weights(in_hbm, out_hbm, in_ref, out_ref, sems)
    own = block_ref.shape[1] // 2
    for g in range(block_ref.shape[0]):
        pair_ref[...] = block_ref[g].astype(F32)
        acts_ref[g * own : (g + 1) * own] = pair_ref[:own]
        cots_ref[g * own : (g + 1) * own] = pair_ref[own:]
    cots, acts = cots_ref[...].astype(BF16), turned(acts_ref[...])
    pre_ref = acts_ref
    weights.columns_dot(acts, pre_ref)
    shares, share = parts_ref.shape[0], parts_ref.shape[1] // 2
    for k in range(shares):
        parts_ref[k, :share] = pre_ref[k * share : (k + 1) * share].astype(BF16)
    each = shares // sems.shape[1]
    for c, grad in enumerate(weights.rows_dot(cots)):
        for j in range(each):
            parts_ref[c * each + j, share:] = grad[j * share : (j + 1) * share].astype(BF16)


def feature_terms(both_ref, in_hbm, out_hbm, sums_ref, out_ref, in_ref, out_rows_ref, in_rows_ref, pair_ref, sems):
    weights = Weights(out_hbm, in_hbm, out_ref, in_ref, sems)
    share = both_ref.shape[1] // 2
    shares = range(both_ref.shape[0])
    hidden = turned(jnp.concatenate([both_ref[k, :share] for k in shares], axis=0))
    grad = jnp.concatenate([both_ref[k, share:] for k in shares], axis=0)
    weights.columns_dot(hidden, out_rows_ref)
    members, own = sums_ref.shape[0], sums_ref.shape[1] // 2
    rows = in_ref.shape[0] // sems.shape[1]
    each = members // sems.shape[1]
    for c, part in enumerate(weights.rows_dot(grad)):
        in_rows_ref[c * rows : (c + 1) * rows] = part
        for g in range(c * each, (c + 1) * each):
            pair_ref[:own] = out_rows_ref[g * own : (g + 1) * own]
            pair_ref[own:] = in_rows_ref[g * own : (g + 1) * own]
            sums_ref[g] = pair_ref[...].astype(BF16)


def relative(step):
    xh, core = lax.axis_index("xh"), lax.axis_index("core")
    return 2 * (1 - xh if step & 2 else xh) + (1 - core if step & 1 else core)


def unpack(block_hbm, acts_out, cots_out, block_ref, acts_ref, cots_ref, pair_ref, sems):
    groups, members, rows, tokens = block_ref.shape
    own = rows // 2
    copies = [
        pltpu.make_async_copy(block_hbm.at[relative(t)], block_ref.at[t], sems.at[t])
        for t in range(groups)
    ]
    for copy in copies:
        copy.start()
    owner = relative(0)
    for t in range(groups):
        copies[t].wait()
        lanes = slice(t * tokens, (t + 1) * tokens)
        for g in range(members):
            pair_ref[...] = block_ref[t, g].astype(F32)
            cots_ref[g * own : (g + 1) * own] = pair_ref[own:]
        cots_out[:, lanes] = cots_ref[...].astype(BF16)
        for g in range(members // groups):
            pair_ref[...] = block_ref[t, owner * (members // groups) + g].astype(F32)
            acts_ref[g * own : (g + 1) * own] = pair_ref[:own]
        acts_out[:, lanes] = acts_ref[...].astype(BF16)


def weight_grads(factor, acts_ref, cots_ref, both_ref, core_ref, far_ref, far_core_ref, in_ref, out_ref):
    shares, share = both_ref.shape[0], both_ref.shape[1] // 2
    units = shares * share
    own = out_ref.shape[0]
    owner, core = relative(0), lax.axis_index("core")
    pieces = own // share
    acts = acts_ref[...]
    grads = jnp.concatenate(
        [jnp.concatenate([ref[k, share:] for k in range(shares)], axis=0) for ref in (both_ref, core_ref)]
        + [ref[:units] for ref in (far_ref, far_core_ref)],
        axis=1,
    )
    width = 384
    for at in range(0, in_ref.shape[1], width):
        part = grads[at : at + width]
        in_ref[:, at : at + width] = (dot(acts, part, ((1,), (1,))) * factor).astype(BF16)
    at = pl.multiple_of(units + core * own, share)
    hidden = jnp.concatenate(
        [
            jnp.concatenate([ref[owner * pieces + j, :share] for j in range(pieces)], axis=0)
            for ref in (both_ref, core_ref)
        ]
        + [ref[pl.ds(at, own)] for ref in (far_ref, far_core_ref)],
        axis=1,
    )
    for at in range(0, out_ref.shape[1], width):
        part = cots_ref[at : at + width]
        out_ref[:, at : at + width] = (dot(hidden, part, ((1,), (1,))) * factor).astype(BF16)


def call(kernel, name, outs, scratch, n_sems, args, in_hbm, flops, vmem):
    n_bytes = sum(a.size * a.dtype.itemsize for a in args)
    return pl.pallas_call(
        kernel,
        out_shape=outs,
        in_specs=[pl.BlockSpec(memory_space=pltpu.HBM) if i in in_hbm else VMEM for i in range(len(args))],
        out_specs=jax.tree.map(lambda _: VMEM, outs),
        scratch_shapes=[pltpu.VMEM(*s) for s in scratch]
        + ([pltpu.SemaphoreType.DMA(n_sems)] if n_sems else []),
        compiler_params=pltpu.CompilerParams(vmem_limit_bytes=vmem * 2**20),
        cost_estimate=pl.CostEstimate(flops=flops, bytes_accessed=n_bytes, transcendentals=0),
        name=name,
    )(*args)


def spread(local, axes):
    copies = jnp.broadcast_to(local[None], (lax.axis_size(axes), *local.shape))
    return lax.all_to_all(copies, axes, 0, 0, tiled=True)


def body(activations, weight_in, weight_out, cotangent):
    own, tokens = activations.shape
    feats, units = weight_in.shape
    n_gx, n_gy, n_dev = (lax.axis_size(a) for a in (GX, "gy", DEV))
    share = units // n_gy
    pair_rows = (2 * own, tokens)
    products = 4 * feats * units * tokens

    pair = jnp.concatenate([activations, cotangent], axis=0)
    block = lax.all_gather(pair, "z", axis=0, tiled=False)
    block = lax.all_gather(block, "xl", axis=0, tiled=True)
    block_all = lax.all_gather(block, DEV, axis=0, tiled=False)

    weight = (weight_in.shape, BF16)
    rows = ((feats, tokens), F32)
    parts = call(
        unit_terms,
        "unit_terms",
        jax.ShapeDtypeStruct((n_gy, 2 * share, tokens), BF16),
        [weight, weight, rows, rows, (pair_rows, F32)],
        (2, 4),
        (block, weight_in, weight_out),
        (1, 2),
        products,
        62,
    )
    parts = lax.all_to_all(parts, "gy", 0, 0, tiled=True)
    total = jnp.sum(parts.astype(F32), axis=0)
    pre, grad_hidden = total[:share], total[share:]
    hidden = jax.nn.silu(pre).astype(BF16)
    grad_pre = (grad_hidden * silu_slope(pre)).astype(BF16)
    both = spread(jnp.concatenate([hidden, grad_pre], axis=0), "gy").reshape(n_gy, 2 * share, tokens)
    swap = [(0, 1), (1, 0)]
    near = lax.axis_index("xh")
    half = lax.dynamic_slice_in_dim(both, (1 - near) * (n_gy // 2), n_gy // 2, 0)[:, :share]
    far = jnp.concatenate([both[:, share:].reshape(units, tokens), half.reshape(units // 2, tokens)])
    far = lax.ppermute(far, "xh", swap)
    both_core = lax.ppermute(both, "core", swap)
    far_core = lax.ppermute(far, "core", swap)

    sums = call(
        feature_terms,
        "feature_terms",
        jax.ShapeDtypeStruct((n_gx, *pair_rows), BF16),
        [weight, weight, rows, rows, (pair_rows, F32)],
        (2, 4),
        (both, weight_in, weight_out),
        (1, 2),
        products,
        62,
    )
    sums = lax.all_to_all(sums, GX, 0, 0, tiled=True)
    sums = jnp.sum(sums.astype(F32), axis=0).astype(BF16)

    acts_own, cots_all = call(
        unpack,
        "unpack",
        (
            jax.ShapeDtypeStruct((feats // n_dev, n_dev * tokens), BF16),
            jax.ShapeDtypeStruct((feats, n_dev * tokens), BF16),
        ),
        [
            (block_all.shape, BF16),
            ((feats // n_dev, tokens), F32),
            ((feats, tokens), F32),
            (pair_rows, F32),
        ],
        (n_dev,),
        (block_all,),
        (0,),
        products,
        62,
    )
    grads = call(
        functools.partial(weight_grads, 1.0 / math.sqrt(n_dev * tokens)),
        "weight_grads",
        (
            jax.ShapeDtypeStruct((feats // n_dev, units), BF16),
            jax.ShapeDtypeStruct((units // n_dev, feats), BF16),
        ),
        [],
        (),
        (acts_own, cots_all, both, both_core, far, far_core),
        (),
        products,
        32,
    )
    return (sums[:own], sums[own:], *grads)


def solution(mesh):
    shape = mesh.devices.shape
    fine = Mesh(
        mesh.devices.reshape(2, shape[0] // 2, shape[1], 2, shape[2] // 2),
        ("xl", "z", "gy", "xh", "core"),
    )
    return jax.shard_map(
        body,
        mesh=fine,
        in_specs=(P(("gy", *GX), DEV), P("gy", GX), P(GX, "gy"), P(("gy", *GX), DEV)),
        out_specs=(P(("gy", *GX), DEV), P(("gy", *GX), DEV), P(("gy", *DEV), GX), P((*GX, *DEV), "gy")),
        check_vma=False,
    )
```

```python
import functools
import math

import jax
import jax.numpy as jnp
from jax import lax
from jax.experimental import pallas as pl
from jax.experimental.pallas import tpu as pltpu
from jax.sharding import Mesh, PartitionSpec as P

F32 = jnp.float32
BF16 = jnp.bfloat16
GX = ("xl", "z")
DEV = ("xh", "core")
VMEM = pl.BlockSpec(memory_space=pltpu.VMEM)


def silu_slope(pre):
    sig = jax.nn.sigmoid(pre)
    return sig * (1.0 + pre * (1.0 - sig))


def dot(left, right, contract):
    return lax.dot_general(left, right, (contract, ((), ())), preferred_element_type=F32)


def turned(right):
    return right.astype(F32).T.astype(BF16)


class Weights:
    def __init__(self, columns_hbm, rows_hbm, columns_ref, rows_ref, sems):
        n = sems.shape[1]
        self.columns_ref, self.rows_ref = columns_ref, rows_ref
        self.column_parts = [pl.ds(c * (columns_ref.shape[1] // 3), columns_ref.shape[1] // 3) for c in range(3)]
        self.row_parts = [pl.ds(c * (rows_ref.shape[0] // n), rows_ref.shape[0] // n) for c in range(n)]
        self.coming = [
            pltpu.make_async_copy(columns_hbm.at[:, part], columns_ref.at[:, part], sems.at[0, c])
            for c, part in enumerate(self.column_parts)
        ] + [
            pltpu.make_async_copy(rows_hbm.at[part], rows_ref.at[part], sems.at[1, c])
            for c, part in enumerate(self.row_parts)
        ]
        self.ahead = 2
        self.taken = 0
        for copy in self.coming[: self.ahead]:
            copy.start()

    def take(self):
        self.coming[self.taken].wait()
        if self.taken + self.ahead < len(self.coming):
            self.coming[self.taken + self.ahead].start()
        self.taken += 1

    def columns_dot(self, left, to_ref):
        for part in self.column_parts:
            self.take()
            to_ref[part] = dot(left, self.columns_ref[:, part], ((1,), (0,))).T

    def rows_dot(self, right):
        for part in self.row_parts:
            self.take()
            yield dot(self.rows_ref[part], right, ((1,), (0,)))


def unit_terms(
    block_hbm, in_hbm, out_hbm, parts_hbm,
    block_ref, parts_ref, in_ref, out_ref, acts_ref, cots_ref, pair_ref, sems, own_sems,
):
    load = pltpu.make_async_copy(block_hbm, block_ref, own_sems.at[0])
    load.start()
    weights = Weights(in_hbm, out_hbm, in_ref, out_ref, sems)
    own = block_ref.shape[1] // 2
    load.wait()
    for g in range(block_ref.shape[0]):
        pair_ref[...] = block_ref[g].astype(F32)
        acts_ref[g * own : (g + 1) * own] = pair_ref[:own]
        cots_ref[g * own : (g + 1) * own] = pair_ref[own:]
    cots, acts = cots_ref[...].astype(BF16), turned(acts_ref[...])
    pre_ref = acts_ref
    weights.columns_dot(acts, pre_ref)
    shares, share = parts_ref.shape[0], parts_ref.shape[1] // 2
    for k in range(shares):
        parts_ref[k, :share] = pre_ref[k * share : (k + 1) * share].astype(BF16)
    each = shares // sems.shape[1]
    stores = []
    for c, grad in enumerate(weights.rows_dot(cots)):
        for j in range(each):
            parts_ref[c * each + j, share:] = grad[j * share : (j + 1) * share].astype(BF16)
        part = pl.ds(c * each, each)
        stores.append(pltpu.make_async_copy(parts_ref.at[part], parts_hbm.at[part], own_sems.at[1 + c]))
        stores[-1].start()
    for store in stores:
        store.wait()


def feature_terms(
    both_hbm, in_hbm, out_hbm, sums_hbm,
    both_ref, sums_ref, out_ref, in_ref, out_rows_ref, in_rows_ref, pair_ref, sems, own_sems,
):
    load = pltpu.make_async_copy(both_hbm, both_ref, own_sems.at[0])
    load.start()
    weights = Weights(out_hbm, in_hbm, out_ref, in_ref, sems)
    share = both_ref.shape[1] // 2
    shares = range(both_ref.shape[0])
    load.wait()
    hidden = turned(jnp.concatenate([both_ref[k, :share] for k in shares], axis=0))
    grad = jnp.concatenate([both_ref[k, share:] for k in shares], axis=0)
    weights.columns_dot(hidden, out_rows_ref)
    members, own = sums_ref.shape[0], sums_ref.shape[1] // 2
    rows = in_ref.shape[0] // sems.shape[1]
    each = members // sems.shape[1]
    stores = []
    for c, part in enumerate(weights.rows_dot(grad)):
        in_rows_ref[c * rows : (c + 1) * rows] = part
        for g in range(c * each, (c + 1) * each):
            pair_ref[:own] = out_rows_ref[g * own : (g + 1) * own]
            pair_ref[own:] = in_rows_ref[g * own : (g + 1) * own]
            sums_ref[g] = pair_ref[...].astype(BF16)
        span = pl.ds(c * each, each)
        stores.append(pltpu.make_async_copy(sums_ref.at[span], sums_hbm.at[span], own_sems.at[1 + c]))
        stores[-1].start()
    for store in stores:
        store.wait()


def relative(step):
    xh, core = lax.axis_index("xh"), lax.axis_index("core")
    return 2 * (1 - xh if step & 2 else xh) + (1 - core if step & 1 else core)


def unpack(block_hbm, unused_hbm, acts_out, cots_out, block_ref, acts_ref, cots_ref, pair_ref, sems):
    groups, members, rows, tokens = block_ref.shape
    own = rows // 2
    copies = [
        pltpu.make_async_copy(block_hbm.at[relative(t)], block_ref.at[t], sems.at[t])
        for t in range(groups)
    ]
    for copy in copies:
        copy.start()
    owner = relative(0)
    for t in range(groups):
        copies[t].wait()
        lanes = slice(t * tokens, (t + 1) * tokens)
        for g in range(members):
            pair_ref[...] = block_ref[t, g].astype(F32)
            cots_ref[g * own : (g + 1) * own] = pair_ref[own:]
        cots_out[:, lanes] = cots_ref[...].astype(BF16)
        for g in range(members // groups):
            pair_ref[...] = block_ref[t, owner * (members // groups) + g].astype(F32)
            acts_ref[g * own : (g + 1) * own] = pair_ref[:own]
        acts_out[:, lanes] = acts_ref[...].astype(BF16)


def weight_grads(factor, acts_ref, cots_ref, both_ref, core_ref, far_ref, far_core_ref, in_ref, out_ref):
    shares, share = both_ref.shape[0], both_ref.shape[1] // 2
    units = shares * share
    own = out_ref.shape[0]
    owner, core = relative(0), lax.axis_index("core")
    pieces = own // share
    acts = acts_ref[...]
    grads = jnp.concatenate(
        [jnp.concatenate([ref[k, share:] for k in range(shares)], axis=0) for ref in (both_ref, core_ref)]
        + [ref[:units] for ref in (far_ref, far_core_ref)],
        axis=1,
    )
    width = 384
    for at in range(0, in_ref.shape[1], width):
        part = grads[at : at + width]
        in_ref[:, at : at + width] = (dot(acts, part, ((1,), (1,))) * factor).astype(BF16)
    at = pl.multiple_of(units + core * own, share)
    hidden = jnp.concatenate(
        [
            jnp.concatenate([ref[owner * pieces + j, :share] for j in range(pieces)], axis=0)
            for ref in (both_ref, core_ref)
        ]
        + [ref[pl.ds(at, own)] for ref in (far_ref, far_core_ref)],
        axis=1,
    )
    for at in range(0, out_ref.shape[1], width):
        part = cots_ref[at : at + width]
        out_ref[:, at : at + width] = (dot(hidden, part, ((1,), (1,))) * factor).astype(BF16)


def call(kernel, name, outs, scratch, sems, args, in_hbm, flops, vmem, out_space=pltpu.VMEM):
    n_bytes = sum(a.size * a.dtype.itemsize for a in args)
    return pl.pallas_call(
        kernel,
        out_shape=outs,
        in_specs=[pl.BlockSpec(memory_space=pltpu.HBM) if i in in_hbm else VMEM for i in range(len(args))],
        out_specs=jax.tree.map(lambda _: pl.BlockSpec(memory_space=out_space), outs),
        scratch_shapes=[pltpu.VMEM(*s) for s in scratch] + [pltpu.SemaphoreType.DMA(s) for s in sems],
        compiler_params=pltpu.CompilerParams(vmem_limit_bytes=vmem * 2**20),
        cost_estimate=pl.CostEstimate(flops=flops, bytes_accessed=n_bytes, transcendentals=0),
        name=name,
    )(*args)


def spread(local, axes):
    copies = jnp.broadcast_to(local[None], (lax.axis_size(axes), *local.shape))
    return lax.all_to_all(copies, axes, 0, 0, tiled=True)


def body(activations, weight_in, weight_out, cotangent):
    own, tokens = activations.shape
    feats, units = weight_in.shape
    n_gx, n_gy, n_dev = (lax.axis_size(a) for a in (GX, "gy", DEV))
    share = units // n_gy
    pair_rows = (2 * own, tokens)
    products = 4 * feats * units * tokens

    pair = jnp.concatenate([activations, cotangent], axis=0)
    block = lax.all_gather(pair, "z", axis=0, tiled=False)
    block = lax.all_gather(block, "xl", axis=0, tiled=True)
    block_all = lax.all_gather(block, DEV, axis=0, tiled=False)

    weight = (weight_in.shape, BF16)
    rows = ((feats, tokens), F32)
    parts = call(
        unit_terms,
        "unit_terms",
        jax.ShapeDtypeStruct((n_gy, 2 * share, tokens), BF16),
        [((n_gx, *pair_rows), BF16), ((n_gy, 2 * share, tokens), BF16), weight, weight, rows, rows, (pair_rows, F32)],
        [(2, 4), (5,)],
        (block, weight_in, weight_out),
        (0, 1, 2),
        products,
        62,
        pltpu.HBM,
    )
    parts = lax.all_to_all(parts, "gy", 0, 0, tiled=True)
    total = jnp.sum(parts.astype(F32), axis=0)
    pre, grad_hidden = total[:share], total[share:]
    hidden = jax.nn.silu(pre).astype(BF16)
    grad_pre = (grad_hidden * silu_slope(pre)).astype(BF16)
    both = spread(jnp.concatenate([hidden, grad_pre], axis=0), "gy").reshape(n_gy, 2 * share, tokens)
    swap = [(0, 1), (1, 0)]
    near = lax.axis_index("xh")
    half = lax.dynamic_slice_in_dim(both, (1 - near) * (n_gy // 2), n_gy // 2, 0)[:, :share]
    far = jnp.concatenate([both[:, share:].reshape(units, tokens), half.reshape(units // 2, tokens)])
    far = lax.ppermute(far, "xh", swap)
    both_core = lax.ppermute(both, "core", swap)
    far_core = lax.ppermute(far, "core", swap)

    sums = call(
        feature_terms,
        "feature_terms",
        jax.ShapeDtypeStruct((n_gx, *pair_rows), BF16),
        [((n_gy, 2 * share, tokens), BF16), ((n_gx, *pair_rows), BF16), weight, weight, rows, rows, (pair_rows, F32)],
        [(2, 4), (5,)],
        (both, weight_in, weight_out),
        (0, 1, 2),
        products,
        62,
        pltpu.HBM,
    )
    sums = lax.all_to_all(sums, GX, 0, 0, tiled=True)
    sums = jnp.sum(sums.astype(F32), axis=0).astype(BF16)

    acts_own, cots_all = call(
        unpack,
        "unpack",
        (
            jax.ShapeDtypeStruct((feats // n_dev, n_dev * tokens), BF16),
            jax.ShapeDtypeStruct((feats, n_dev * tokens), BF16),
        ),
        [
            (block_all.shape, BF16),
            ((feats // n_dev, tokens), F32),
            ((feats, tokens), F32),
            (pair_rows, F32),
        ],
        [(n_dev,)],
        (block_all, both_core),
        (0, 1),
        32 * products,
        62,
    )
    grads = call(
        functools.partial(weight_grads, 1.0 / math.sqrt(n_dev * tokens)),
        "weight_grads",
        (
            jax.ShapeDtypeStruct((feats // n_dev, units), BF16),
            jax.ShapeDtypeStruct((units // n_dev, feats), BF16),
        ),
        [],
        [],
        (acts_own, cots_all, both, both_core, far, far_core),
        (),
        products,
        32,
    )
    return (sums[:own], sums[own:], *grads)


def solution(mesh):
    shape = mesh.devices.shape
    fine = Mesh(
        mesh.devices.reshape(2, shape[0] // 2, shape[1], 2, shape[2] // 2),
        ("xl", "z", "gy", "xh", "core"),
    )
    return jax.shard_map(
        body,
        mesh=fine,
        in_specs=(P(("gy", *GX), DEV), P("gy", GX), P(GX, "gy"), P(("gy", *GX), DEV)),
        out_specs=(P(("gy", *GX), DEV), P(("gy", *GX), DEV), P(("gy", *DEV), GX), P((*GX, *DEV), "gy")),
        check_vma=False,
    )
```

```python
import functools
import math

import jax
import jax.numpy as jnp
from jax import lax
from jax.experimental import pallas as pl
from jax.experimental.pallas import tpu as pltpu
from jax.sharding import Mesh, PartitionSpec as P

F32 = jnp.float32
BF16 = jnp.bfloat16
GX = ("xl", "z")
DEV = ("xh", "core")
VMEM = pl.BlockSpec(memory_space=pltpu.VMEM)


def silu_slope(pre):
    sig = jax.nn.sigmoid(pre)
    return sig * (1.0 + pre * (1.0 - sig))


def dot(left, right, contract):
    return lax.dot_general(left, right, (contract, ((), ())), preferred_element_type=F32)


def turned(right):
    return right.astype(F32).T.astype(BF16)


def columns_dot(left, columns_ref, to_ref):
    width = 384
    for at in range(0, columns_ref.shape[1], width):
        to_ref[at : at + width] = dot(left, columns_ref[:, at : at + width], ((1,), (0,))).T


def unit_terms(
    block_hbm, in_hbm, out_hbm, parts_hbm,
    block_ref, parts_ref, in_ref, out_ref, acts_ref, cots_ref, pair_ref, sems,
):
    load = pltpu.make_async_copy(block_hbm, block_ref, sems.at[0])
    load_in = pltpu.make_async_copy(in_hbm, in_ref, sems.at[1])
    load_out = pltpu.make_async_copy(out_hbm, out_ref, sems.at[2])
    load.start()
    load_in.start()
    own = block_ref.shape[1] // 2
    load.wait()
    load_out.start()
    for g in range(block_ref.shape[0]):
        pair_ref[...] = block_ref[g].astype(F32)
        acts_ref[g * own : (g + 1) * own] = pair_ref[:own]
        cots_ref[g * own : (g + 1) * own] = pair_ref[own:]
    cots, acts = cots_ref[...].astype(BF16), turned(acts_ref[...])
    pre_ref = acts_ref
    load_in.wait()
    columns_dot(acts, in_ref, pre_ref)
    shares, share = parts_ref.shape[0], parts_ref.shape[1] // 2
    for k in range(shares):
        parts_ref[k, :share] = pre_ref[k * share : (k + 1) * share].astype(BF16)
    load_out.wait()
    each = 2
    stores = []
    for k in range(0, shares, each):
        grad = dot(out_ref[k * share : (k + each) * share], cots, ((1,), (0,))).astype(BF16)
        for j in range(each):
            parts_ref[k + j, share:] = grad[j * share : (j + 1) * share]
        part = pl.ds(k, each)
        stores.append(pltpu.make_async_copy(parts_ref.at[part], parts_hbm.at[part], sems.at[3 + k // each]))
        stores[-1].start()
    for store in stores:
        store.wait()


def feature_terms(
    both_hbm, in_hbm, out_hbm, sums_hbm, near_hbm, far_hbm,
    both_ref, sums_ref, in_ref, out_ref, out_rows_ref, in_rows_ref, pair_ref, sems,
):
    shares, share = both_ref.shape[0], both_ref.shape[1] // 2
    load = pltpu.make_async_copy(both_hbm, both_ref, sems.at[0])
    load_in = pltpu.make_async_copy(in_hbm, in_ref, sems.at[10])
    load_out = pltpu.make_async_copy(out_hbm, out_ref, sems.at[1])
    load.start()
    load_in.start()
    quarter, half = near_hbm.shape[0] - shares, far_hbm.shape[0] - shares
    load.wait()
    stores = [
        pltpu.make_async_copy(source, target, sems.at[2 + i])
        for i, (source, target) in enumerate(
            [
                (both_ref.at[:, pl.ds(share, share)], near_hbm.at[pl.ds(0, shares)]),
                (both_ref.at[pl.ds(relative(1) * quarter, quarter), pl.ds(0, share)], near_hbm.at[pl.ds(shares, quarter)]),
                (both_ref.at[:, pl.ds(share, share)], far_hbm.at[pl.ds(0, shares)]),
                (both_ref.at[pl.ds((1 - lax.axis_index("xh")) * half, half), pl.ds(0, share)], far_hbm.at[pl.ds(shares, half)]),
            ]
        )
    ]
    load_out.start()
    for store in stores:
        store.start()
    grad = jnp.concatenate([both_ref[k, share:] for k in range(shares)], axis=0)
    load_in.wait()
    in_rows_ref[...] = dot(in_ref[...], grad, ((1,), (0,)))
    hidden = turned(jnp.concatenate([both_ref[k, :share] for k in range(shares)], axis=0))
    load_out.wait()
    columns_dot(hidden, out_ref, out_rows_ref)
    members, own = sums_ref.shape[0], sums_ref.shape[1] // 2
    each = members // 4
    for c in range(4):
        for g in range(c * each, (c + 1) * each):
            pair_ref[:own] = out_rows_ref[g * own : (g + 1) * own]
            pair_ref[own:] = in_rows_ref[g * own : (g + 1) * own]
            sums_ref[g] = pair_ref[...].astype(BF16)
        span = pl.ds(c * each, each)
        stores.append(pltpu.make_async_copy(sums_ref.at[span], sums_hbm.at[span], sems.at[6 + c]))
        stores[-1].start()
    for store in stores:
        store.wait()


def relative(step):
    xh, core = lax.axis_index("xh"), lax.axis_index("core")
    return 2 * (1 - xh if step & 2 else xh) + (1 - core if step & 1 else core)


def unpack(block_hbm, acts_out, cots_out, block_ref, acts_ref, cots_ref, pair_ref, sems):
    groups, members, rows, tokens = block_ref.shape
    own = rows // 2
    copies = [
        pltpu.make_async_copy(block_hbm.at[relative(t)], block_ref.at[t], sems.at[t])
        for t in range(groups)
    ]
    for copy in copies:
        copy.start()
    owner = relative(0)
    for t in range(groups):
        copies[t].wait()
        lanes = slice(t * tokens, (t + 1) * tokens)
        for g in range(members):
            pair_ref[...] = block_ref[t, g].astype(F32)
            cots_ref[g * own : (g + 1) * own] = pair_ref[own:]
        cots_out[:, lanes] = cots_ref[...].astype(BF16)
        for g in range(members // groups):
            pair_ref[...] = block_ref[t, owner * (members // groups) + g].astype(F32)
            acts_ref[g * own : (g + 1) * own] = pair_ref[:own]
        acts_out[:, lanes] = acts_ref[...].astype(BF16)


def weight_grads(factor, acts_ref, cots_ref, both_ref, near_ref, far_ref, far_near_ref, in_ref, out_ref):
    shares, share = both_ref.shape[0], both_ref.shape[1] // 2
    pieces = out_ref.shape[0] // share
    owner, core = relative(0), lax.axis_index("core")
    others = (near_ref, far_ref, far_near_ref)
    acts = acts_ref[...]
    own_grads = jnp.concatenate([both_ref[k, share:] for k in range(shares)], axis=0)
    grads = jnp.concatenate(
        [own_grads] + [jnp.concatenate([ref[k] for k in range(shares)], axis=0) for ref in others], axis=1
    )
    width = 384
    for at in range(0, in_ref.shape[1], width):
        part = grads[at : at + width]
        in_ref[:, at : at + width] = (dot(acts, part, ((1,), (1,))) * factor).astype(BF16)
    places = (shares, shares + core * pieces, shares + core * pieces)
    own_hidden = jnp.concatenate([both_ref[owner * pieces + j, :share] for j in range(pieces)], axis=0)
    hidden = jnp.concatenate(
        [own_hidden]
        + [
            jnp.concatenate([ref[place + j] for j in range(pieces)], axis=0)
            for ref, place in zip(others, places)
        ],
        axis=1,
    )
    for at in range(0, out_ref.shape[1], width):
        part = cots_ref[at : at + width]
        out_ref[:, at : at + width] = (dot(hidden, part, ((1,), (1,))) * factor).astype(BF16)


def call(kernel, name, outs, scratch, sems, args, in_hbm, flops, vmem, out_hbm=()):
    n_bytes = sum(a.size * a.dtype.itemsize for a in args)
    return pl.pallas_call(
        kernel,
        out_shape=outs,
        in_specs=[pl.BlockSpec(memory_space=pltpu.HBM) if i in in_hbm else VMEM for i in range(len(args))],
        out_specs=tuple(pl.BlockSpec(memory_space=pltpu.HBM) if i in out_hbm else VMEM for i in range(len(outs))),
        scratch_shapes=[pltpu.VMEM(*s) for s in scratch] + [pltpu.SemaphoreType.DMA(s) for s in sems],
        compiler_params=pltpu.CompilerParams(vmem_limit_bytes=vmem * 2**20),
        cost_estimate=pl.CostEstimate(flops=flops, bytes_accessed=n_bytes, transcendentals=0),
        name=name,
    )(*args)


def spread(local, axes):
    copies = jnp.broadcast_to(local[None], (lax.axis_size(axes), *local.shape))
    return lax.all_to_all(copies, axes, 0, 0, tiled=True)


def body(activations, weight_in, weight_out, cotangent):
    own, tokens = activations.shape
    feats, units = weight_in.shape
    n_gx, n_gy, n_dev = (lax.axis_size(a) for a in (GX, "gy", DEV))
    share = units // n_gy
    pair_rows = (2 * own, tokens)
    products = 4 * feats * units * tokens

    pair = jnp.concatenate([activations, cotangent], axis=0)
    block = lax.all_gather(pair, "z", axis=0, tiled=False)
    block = lax.all_gather(block, "xl", axis=0, tiled=True)
    block_all = lax.all_gather(block, DEV, axis=0, tiled=False)

    weight = (weight_in.shape, BF16)
    rows = ((feats, tokens), F32)
    (parts,) = call(
        unit_terms,
        "unit_terms",
        (jax.ShapeDtypeStruct((n_gy, 2 * share, tokens), BF16),),
        [((n_gx, *pair_rows), BF16), ((n_gy, 2 * share, tokens), BF16), weight, weight, rows, rows, (pair_rows, F32)],
        [(3 + n_gy // 2,)],
        (block, weight_in, weight_out),
        (0, 1, 2),
        products,
        62,
        (0,),
    )
    parts = lax.all_to_all(parts, "gy", 0, 0, tiled=True)
    total = jnp.sum(parts.astype(F32), axis=0)
    pre, grad_hidden = total[:share], total[share:]
    hidden = jax.nn.silu(pre).astype(BF16)
    grad_pre = (grad_hidden * silu_slope(pre)).astype(BF16)
    both = spread(jnp.concatenate([hidden, grad_pre], axis=0), "gy").reshape(n_gy, 2 * share, tokens)
    sums, near, far = call(
        feature_terms,
        "feature_terms",
        (
            jax.ShapeDtypeStruct((n_gx, *pair_rows), BF16),
            jax.ShapeDtypeStruct((n_gy + n_gy // n_dev, share, tokens), BF16),
            jax.ShapeDtypeStruct((n_gy + n_gy // 2, share, tokens), BF16),
        ),
        [((n_gy, 2 * share, tokens), BF16), ((n_gx, *pair_rows), BF16), weight, weight, rows, rows, (pair_rows, F32)],
        [(11,)],
        (both, weight_in, weight_out),
        (0, 1, 2),
        products,
        62,
        (0, 1, 2),
    )
    swap = [(0, 1), (1, 0)]
    far = lax.ppermute(far, "xh", swap)
    near = lax.ppermute(near, "core", swap)
    far_near = lax.ppermute(far, "core", swap)
    sums = lax.all_to_all(sums, GX, 0, 0, tiled=True)
    sums = jnp.sum(sums.astype(F32), axis=0).astype(BF16)

    acts_own, cots_all = call(
        unpack,
        "unpack",
        (
            jax.ShapeDtypeStruct((feats // n_dev, n_dev * tokens), BF16),
            jax.ShapeDtypeStruct((feats, n_dev * tokens), BF16),
        ),
        [
            (block_all.shape, BF16),
            ((feats // n_dev, tokens), F32),
            ((feats, tokens), F32),
            (pair_rows, F32),
        ],
        [(n_dev,)],
        (block_all,),
        (0,),
        products,
        62,
    )
    grads = call(
        functools.partial(weight_grads, 1.0 / math.sqrt(n_dev * tokens)),
        "weight_grads",
        (
            jax.ShapeDtypeStruct((feats // n_dev, units), BF16),
            jax.ShapeDtypeStruct((units // n_dev, feats), BF16),
        ),
        [],
        [],
        (acts_own, cots_all, both, near, far, far_near),
        (),
        products,
        32,
    )
    return (sums[:own], sums[own:], *grads)


def solution(mesh):
    shape = mesh.devices.shape
    fine = Mesh(
        mesh.devices.reshape(2, shape[0] // 2, shape[1], 2, shape[2] // 2),
        ("xl", "z", "gy", "xh", "core"),
    )
    return jax.shard_map(
        body,
        mesh=fine,
        in_specs=(P(("gy", *GX), DEV), P("gy", GX), P(GX, "gy"), P(("gy", *GX), DEV)),
        out_specs=(P(("gy", *GX), DEV), P(("gy", *GX), DEV), P(("gy", *DEV), GX), P((*GX, *DEV), "gy")),
        check_vma=False,
    )
```

```python
import functools
import math

import jax
import jax.numpy as jnp
from jax import lax
from jax.experimental import pallas as pl
from jax.experimental.pallas import tpu as pltpu
from jax.sharding import Mesh, PartitionSpec as P

F32 = jnp.float32
BF16 = jnp.bfloat16
GX = ("xl", "z")
DEV = ("xh", "core")
VMEM = pl.BlockSpec(memory_space=pltpu.VMEM)


def silu_slope(pre):
    sig = jax.nn.sigmoid(pre)
    return sig * (1.0 + pre * (1.0 - sig))


def dot(left, right, contract):
    return lax.dot_general(left, right, (contract, ((), ())), preferred_element_type=F32)


def turned(right):
    return right.astype(F32).T.astype(BF16)


def columns_dot(left, columns_ref, to_ref):
    width = 384
    for at in range(0, columns_ref.shape[1], width):
        to_ref[at : at + width] = dot(left, columns_ref[:, at : at + width], ((1,), (0,))).T


def unit_terms(
    block_hbm, in_hbm, out_hbm, parts_hbm,
    block_ref, parts_ref, in_ref, out_ref, acts_ref, cots_ref, pair_ref, sems,
):
    load = pltpu.make_async_copy(block_hbm, block_ref, sems.at[0])
    load_in = pltpu.make_async_copy(in_hbm, in_ref, sems.at[1])
    load_out = pltpu.make_async_copy(out_hbm, out_ref, sems.at[2])
    load.start()
    load_in.start()
    own = block_ref.shape[1] // 2
    load.wait()
    load_out.start()
    for g in range(block_ref.shape[0]):
        pair_ref[...] = block_ref[g].astype(F32)
        acts_ref[g * own : (g + 1) * own] = pair_ref[:own]
        cots_ref[g * own : (g + 1) * own] = pair_ref[own:]
    cots, acts = cots_ref[...].astype(BF16), turned(acts_ref[...])
    pre_ref = acts_ref
    load_in.wait()
    columns_dot(acts, in_ref, pre_ref)
    shares, share = parts_ref.shape[0], parts_ref.shape[1] // 2
    for k in range(shares):
        parts_ref[k, :share] = pre_ref[k * share : (k + 1) * share].astype(BF16)
    load_out.wait()
    each = 2
    stores = []
    for k in range(0, shares, each):
        grad = dot(out_ref[k * share : (k + each) * share], cots, ((1,), (0,))).astype(BF16)
        for j in range(each):
            parts_ref[k + j, share:] = grad[j * share : (j + 1) * share]
        part = pl.ds(k, each)
        stores.append(pltpu.make_async_copy(parts_ref.at[part], parts_hbm.at[part], sems.at[3 + k // each]))
        stores[-1].start()
    for store in stores:
        store.wait()


def feature_terms(
    both_hbm, in_hbm, out_hbm, sums_hbm, near_hbm, far_hbm,
    both_ref, sums_ref, in_ref, out_ref, out_rows_ref, in_rows_ref, pair_ref, sems,
):
    shares, share = both_ref.shape[0], both_ref.shape[1] // 2
    load = pltpu.make_async_copy(both_hbm, both_ref, sems.at[0])
    load_in = pltpu.make_async_copy(in_hbm, in_ref, sems.at[10])
    load_out = pltpu.make_async_copy(out_hbm, out_ref, sems.at[1])
    load.start()
    load_in.start()
    quarter, half = near_hbm.shape[0] - shares, far_hbm.shape[0] - shares
    load.wait()
    stores = [
        pltpu.make_async_copy(source, target, sems.at[2 + i])
        for i, (source, target) in enumerate(
            [
                (both_ref.at[:, pl.ds(share, share)], near_hbm.at[pl.ds(0, shares)]),
                (both_ref.at[pl.ds(relative(1) * quarter, quarter), pl.ds(0, share)], near_hbm.at[pl.ds(shares, quarter)]),
                (both_ref.at[:, pl.ds(share, share)], far_hbm.at[pl.ds(0, shares)]),
                (both_ref.at[pl.ds((1 - lax.axis_index("xh")) * half, half), pl.ds(0, share)], far_hbm.at[pl.ds(shares, half)]),
            ]
        )
    ]
    load_out.start()
    for store in stores:
        store.start()
    grad = jnp.concatenate([both_ref[k, share:] for k in range(shares)], axis=0)
    load_in.wait()
    in_rows_ref[...] = dot(in_ref[...], grad, ((1,), (0,)))
    hidden = turned(jnp.concatenate([both_ref[k, :share] for k in range(shares)], axis=0))
    load_out.wait()
    columns_dot(hidden, out_ref, out_rows_ref)
    members, own = sums_ref.shape[0], sums_ref.shape[1] // 2
    each = members // 4
    for c in range(4):
        for g in range(c * each, (c + 1) * each):
            pair_ref[:own] = out_rows_ref[g * own : (g + 1) * own]
            pair_ref[own:] = in_rows_ref[g * own : (g + 1) * own]
            sums_ref[g] = pair_ref[...].astype(BF16)
        span = pl.ds(c * each, each)
        stores.append(pltpu.make_async_copy(sums_ref.at[span], sums_hbm.at[span], sems.at[6 + c]))
        stores[-1].start()
    for store in stores:
        store.wait()


def relative(step):
    xh, core = lax.axis_index("xh"), lax.axis_index("core")
    return 2 * (1 - xh if step & 2 else xh) + (1 - core if step & 1 else core)


def unpack(block_hbm, acts_out, cots_out, block_ref, acts_ref, cots_ref, pair_ref, sems):
    groups, members, rows, tokens = block_ref.shape
    own = rows // 2
    copies = [
        pltpu.make_async_copy(block_hbm.at[relative(t)], block_ref.at[t], sems.at[t])
        for t in range(groups)
    ]
    for copy in copies:
        copy.start()
    owner = relative(0)
    for t in range(groups):
        copies[t].wait()
        lanes = slice(t * tokens, (t + 1) * tokens)
        for g in range(members):
            pair_ref[...] = block_ref[t, g].astype(F32)
            cots_ref[g * own : (g + 1) * own] = pair_ref[own:]
        cots_out[:, lanes] = cots_ref[...].astype(BF16)
        for g in range(members // groups):
            pair_ref[...] = block_ref[t, owner * (members // groups) + g].astype(F32)
            acts_ref[g * own : (g + 1) * own] = pair_ref[:own]
        acts_out[:, lanes] = acts_ref[...].astype(BF16)


def forward(far_ref, after_hbm, out_ref, sems):
    pieces = far_ref.shape[0] - out_ref.shape[0]
    shares = out_ref.shape[0] - pieces
    other = shares + (1 - lax.axis_index("core")) * pieces
    copies = [
        pltpu.make_async_copy(far_ref.at[pl.ds(0, shares)], out_ref.at[pl.ds(0, shares)], sems.at[0]),
        pltpu.make_async_copy(far_ref.at[pl.ds(other, pieces)], out_ref.at[pl.ds(shares, pieces)], sems.at[1]),
    ]
    for copy in copies:
        copy.start()
    for copy in copies:
        copy.wait()


def weight_grads(factor, acts_ref, cots_ref, both_ref, near_ref, far_ref, far_near_ref, in_ref, out_ref):
    shares, share = both_ref.shape[0], both_ref.shape[1] // 2
    pieces = out_ref.shape[0] // share
    owner, core = relative(0), lax.axis_index("core")
    others = (near_ref, far_ref, far_near_ref)
    acts = acts_ref[...]
    own_grads = jnp.concatenate([both_ref[k, share:] for k in range(shares)], axis=0)
    grads = jnp.concatenate(
        [own_grads] + [jnp.concatenate([ref[k] for k in range(shares)], axis=0) for ref in others], axis=1
    )
    width = 384
    for at in range(0, in_ref.shape[1], width):
        part = grads[at : at + width]
        in_ref[:, at : at + width] = (dot(acts, part, ((1,), (1,))) * factor).astype(BF16)
    places = (shares, shares + core * pieces, shares)
    own_hidden = jnp.concatenate([both_ref[owner * pieces + j, :share] for j in range(pieces)], axis=0)
    hidden = jnp.concatenate(
        [own_hidden]
        + [
            jnp.concatenate([ref[place + j] for j in range(pieces)], axis=0)
            for ref, place in zip(others, places)
        ],
        axis=1,
    )
    for at in range(0, out_ref.shape[1], width):
        part = cots_ref[at : at + width]
        out_ref[:, at : at + width] = (dot(hidden, part, ((1,), (1,))) * factor).astype(BF16)


def call(kernel, name, outs, scratch, sems, args, in_hbm, flops, vmem, out_hbm=()):
    n_bytes = sum(a.size * a.dtype.itemsize for a in args)
    return pl.pallas_call(
        kernel,
        out_shape=outs,
        in_specs=[pl.BlockSpec(memory_space=pltpu.HBM) if i in in_hbm else VMEM for i in range(len(args))],
        out_specs=tuple(pl.BlockSpec(memory_space=pltpu.HBM) if i in out_hbm else VMEM for i in range(len(outs))),
        scratch_shapes=[pltpu.VMEM(*s) for s in scratch] + [pltpu.SemaphoreType.DMA(s) for s in sems],
        compiler_params=pltpu.CompilerParams(vmem_limit_bytes=vmem * 2**20),
        cost_estimate=pl.CostEstimate(flops=flops, bytes_accessed=n_bytes, transcendentals=0),
        name=name,
    )(*args)


def spread(local, axes):
    copies = jnp.broadcast_to(local[None], (lax.axis_size(axes), *local.shape))
    return lax.all_to_all(copies, axes, 0, 0, tiled=True)


def body(activations, weight_in, weight_out, cotangent):
    own, tokens = activations.shape
    feats, units = weight_in.shape
    n_gx, n_gy, n_dev = (lax.axis_size(a) for a in (GX, "gy", DEV))
    share = units // n_gy
    pair_rows = (2 * own, tokens)
    products = 4 * feats * units * tokens

    pair = jnp.concatenate([activations, cotangent], axis=0)
    block = lax.all_gather(pair, "z", axis=0, tiled=False)
    block = lax.all_gather(block, "xl", axis=0, tiled=True)
    block_all = lax.all_gather(block, DEV, axis=0, tiled=False)

    weight = (weight_in.shape, BF16)
    rows = ((feats, tokens), F32)
    (parts,) = call(
        unit_terms,
        "unit_terms",
        (jax.ShapeDtypeStruct((n_gy, 2 * share, tokens), BF16),),
        [((n_gx, *pair_rows), BF16), ((n_gy, 2 * share, tokens), BF16), weight, weight, rows, rows, (pair_rows, F32)],
        [(3 + n_gy // 2,)],
        (block, weight_in, weight_out),
        (0, 1, 2),
        products,
        62,
        (0,),
    )
    parts = lax.all_to_all(parts, "gy", 0, 0, tiled=True)
    total = jnp.sum(parts.astype(F32), axis=0)
    pre, grad_hidden = total[:share], total[share:]
    hidden = jax.nn.silu(pre).astype(BF16)
    grad_pre = (grad_hidden * silu_slope(pre)).astype(BF16)
    both = spread(jnp.concatenate([hidden, grad_pre], axis=0), "gy").reshape(n_gy, 2 * share, tokens)
    sums, near, far = call(
        feature_terms,
        "feature_terms",
        (
            jax.ShapeDtypeStruct((n_gx, *pair_rows), BF16),
            jax.ShapeDtypeStruct((n_gy + n_gy // n_dev, share, tokens), BF16),
            jax.ShapeDtypeStruct((n_gy + n_gy // 2, share, tokens), BF16),
        ),
        [((n_gy, 2 * share, tokens), BF16), ((n_gx, *pair_rows), BF16), weight, weight, rows, rows, (pair_rows, F32)],
        [(11,)],
        (both, weight_in, weight_out),
        (0, 1, 2),
        products,
        62,
        (0, 1, 2),
    )
    swap = [(0, 1), (1, 0)]
    far = lax.ppermute(far, "xh", swap)
    near = lax.ppermute(near, "core", swap)
    (far_near,) = call(
        forward, "forward", (jax.ShapeDtypeStruct(near.shape, BF16),), [], [(2,)], (far, near), (1,), 0, 32
    )
    far_near = lax.ppermute(far_near, "core", swap)
    sums = lax.all_to_all(sums, GX, 0, 0, tiled=True)
    sums = jnp.sum(sums.astype(F32), axis=0).astype(BF16)

    acts_own, cots_all = call(
        unpack,
        "unpack",
        (
            jax.ShapeDtypeStruct((feats // n_dev, n_dev * tokens), BF16),
            jax.ShapeDtypeStruct((feats, n_dev * tokens), BF16),
        ),
        [
            (block_all.shape, BF16),
            ((feats // n_dev, tokens), F32),
            ((feats, tokens), F32),
            (pair_rows, F32),
        ],
        [(n_dev,)],
        (block_all,),
        (0,),
        products,
        40,
    )
    grads = call(
        functools.partial(weight_grads, 1.0 / math.sqrt(n_dev * tokens)),
        "weight_grads",
        (
            jax.ShapeDtypeStruct((feats // n_dev, units), BF16),
            jax.ShapeDtypeStruct((units // n_dev, feats), BF16),
        ),
        [],
        [],
        (acts_own, cots_all, both, near, far, far_near),
        (),
        products,
        32,
    )
    return (sums[:own], sums[own:], *grads)


def solution(mesh):
    shape = mesh.devices.shape
    fine = Mesh(
        mesh.devices.reshape(2, shape[0] // 2, shape[1], 2, shape[2] // 2),
        ("xl", "z", "gy", "xh", "core"),
    )
    return jax.shard_map(
        body,
        mesh=fine,
        in_specs=(P(("gy", *GX), DEV), P("gy", GX), P(GX, "gy"), P(("gy", *GX), DEV)),
        out_specs=(P(("gy", *GX), DEV), P(("gy", *GX), DEV), P(("gy", *DEV), GX), P((*GX, *DEV), "gy")),
        check_vma=False,
    )
```

```python
import functools
import math

import jax
import jax.numpy as jnp
from jax import lax
from jax.experimental import pallas as pl
from jax.experimental.pallas import tpu as pltpu
from jax.sharding import Mesh, PartitionSpec as P

F32 = jnp.float32
BF16 = jnp.bfloat16
GX = ("xl", "z")
DEV = ("xh", "core")
VMEM = pl.BlockSpec(memory_space=pltpu.VMEM)


def silu_slope(pre):
    sig = jax.nn.sigmoid(pre)
    return sig * (1.0 + pre * (1.0 - sig))


def dot(left, right, contract):
    return lax.dot_general(left, right, (contract, ((), ())), preferred_element_type=F32)


def turned(right):
    return right.astype(F32).T.astype(BF16)


def columns_dot(left, columns_ref, to_ref):
    width = 384
    for at in range(0, columns_ref.shape[1], width):
        to_ref[at : at + width] = dot(left, columns_ref[:, at : at + width], ((1,), (0,))).T


def unit_terms(
    block_hbm, in_hbm, out_hbm, parts_hbm, own_hbm, near_hbm, far_hbm,
    block_ref, parts_ref, features_ref, in_ref, out_ref, acts_ref, cots_ref, pair_ref, sems, feature_sems,
):
    load = pltpu.make_async_copy(block_hbm, block_ref, sems.at[0])
    load_in = pltpu.make_async_copy(in_hbm, in_ref, sems.at[1])
    load_out = pltpu.make_async_copy(out_hbm, out_ref, sems.at[2])
    load.start()
    load_in.start()
    own = block_ref.shape[1] // 2
    load.wait()
    load_out.start()
    for g in range(block_ref.shape[0]):
        pair_ref[...] = block_ref[g].astype(F32)
        acts_ref[g * own : (g + 1) * own] = pair_ref[:own]
        cots_ref[g * own : (g + 1) * own] = pair_ref[own:]
    cots, acts = cots_ref[...].astype(BF16), turned(acts_ref[...])
    pieces = features_ref.shape[0] // 2
    rows = features_ref.shape[1]
    for k in range(pieces):
        features_ref[k] = cots_ref[k * rows : (k + 1) * rows].astype(BF16)
        features_ref[pieces + k] = acts_ref[k * rows : (k + 1) * rows].astype(BF16)
    quarter, half = near_hbm.shape[0] - pieces, far_hbm.shape[0] - pieces
    stores = []
    for i, (target, start, count) in enumerate(
        [
            (near_hbm, relative(1) * quarter, quarter),
            (far_hbm, (1 - lax.axis_index("xh")) * half, half),
            (own_hbm, relative(0) * quarter, quarter),
        ]
    ):
        stores.append(
            pltpu.make_async_copy(features_ref.at[pl.ds(0, pieces)], target.at[pl.ds(0, pieces)], feature_sems.at[2 * i])
        )
        stores.append(
            pltpu.make_async_copy(
                features_ref.at[pl.ds(pieces + start, count)], target.at[pl.ds(pieces, count)], feature_sems.at[2 * i + 1]
            )
        )
    pre_ref = acts_ref
    load_in.wait()
    for store in stores:
        store.start()
    columns_dot(acts, in_ref, pre_ref)
    shares, share = parts_ref.shape[0], parts_ref.shape[1] // 2
    for k in range(shares):
        parts_ref[k, :share] = pre_ref[k * share : (k + 1) * share].astype(BF16)
    load_out.wait()
    each = 2
    for k in range(0, shares, each):
        grad = dot(out_ref[k * share : (k + each) * share], cots, ((1,), (0,))).astype(BF16)
        for j in range(each):
            parts_ref[k + j, share:] = grad[j * share : (j + 1) * share]
        part = pl.ds(k, each)
        stores.append(pltpu.make_async_copy(parts_ref.at[part], parts_hbm.at[part], sems.at[3 + k // each]))
        stores[-1].start()
    for store in stores:
        store.wait()


def activate(parts_ref, near_hbm, far_hbm, copies_ref):
    shares, share = parts_ref.shape[0], parts_ref.shape[1] // 2
    total = parts_ref[0].astype(F32)
    for k in range(1, shares):
        total = total + parts_ref[k].astype(F32)
    pre, grad_hidden = total[:share], total[share:]
    hidden = jax.nn.silu(pre).astype(BF16)
    grad_pre = (grad_hidden * silu_slope(pre)).astype(BF16)
    for k in range(shares):
        copies_ref[k, :share] = hidden
        copies_ref[k, share:] = grad_pre


def feature_terms(
    both_hbm, in_hbm, out_hbm, after_hbm, sums_hbm, near_hbm, far_hbm,
    both_ref, sums_ref, in_ref, out_ref, out_rows_ref, in_rows_ref, pair_ref, sems,
):
    shares, share = both_ref.shape[0], both_ref.shape[1] // 2
    load = pltpu.make_async_copy(both_hbm, both_ref, sems.at[0])
    load_in = pltpu.make_async_copy(in_hbm, in_ref, sems.at[10])
    load_out = pltpu.make_async_copy(out_hbm, out_ref, sems.at[1])
    load.start()
    load_in.start()
    quarter, half = near_hbm.shape[0] - shares, far_hbm.shape[0] - shares
    load.wait()
    stores = [
        pltpu.make_async_copy(source, target, sems.at[2 + i])
        for i, (source, target) in enumerate(
            [
                (both_ref.at[:, pl.ds(share, share)], near_hbm.at[pl.ds(0, shares)]),
                (both_ref.at[pl.ds(relative(1) * quarter, quarter), pl.ds(0, share)], near_hbm.at[pl.ds(shares, quarter)]),
                (both_ref.at[:, pl.ds(share, share)], far_hbm.at[pl.ds(0, shares)]),
                (both_ref.at[pl.ds((1 - lax.axis_index("xh")) * half, half), pl.ds(0, share)], far_hbm.at[pl.ds(shares, half)]),
            ]
        )
    ]
    load_out.start()
    for store in stores:
        store.start()
    grad = jnp.concatenate([both_ref[k, share:] for k in range(shares)], axis=0)
    load_in.wait()
    in_rows_ref[...] = dot(in_ref[...], grad, ((1,), (0,)))
    hidden = turned(jnp.concatenate([both_ref[k, :share] for k in range(shares)], axis=0))
    load_out.wait()
    columns_dot(hidden, out_ref, out_rows_ref)
    members, own = sums_ref.shape[0], sums_ref.shape[1] // 2
    each = members // 4
    for c in range(4):
        for g in range(c * each, (c + 1) * each):
            pair_ref[:own] = out_rows_ref[g * own : (g + 1) * own]
            pair_ref[own:] = in_rows_ref[g * own : (g + 1) * own]
            sums_ref[g] = pair_ref[...].astype(BF16)
        span = pl.ds(c * each, each)
        stores.append(pltpu.make_async_copy(sums_ref.at[span], sums_hbm.at[span], sems.at[6 + c]))
        stores[-1].start()
    for store in stores:
        store.wait()


def relative(step):
    xh, core = lax.axis_index("xh"), lax.axis_index("core")
    return 2 * (1 - xh if step & 2 else xh) + (1 - core if step & 1 else core)


def forward(far_ref, after_hbm, out_ref, sems):
    pieces = far_ref.shape[0] - out_ref.shape[0]
    shares = out_ref.shape[0] - pieces
    other = shares + (1 - lax.axis_index("core")) * pieces
    copies = [
        pltpu.make_async_copy(far_ref.at[pl.ds(0, shares)], out_ref.at[pl.ds(0, shares)], sems.at[0]),
        pltpu.make_async_copy(far_ref.at[pl.ds(other, pieces)], out_ref.at[pl.ds(shares, pieces)], sems.at[1]),
    ]
    for copy in copies:
        copy.start()
    for copy in copies:
        copy.wait()


def weight_grads(
    factor, own_features_ref, near_features_ref, far_features_ref, far_near_features_ref,
    both_ref, near_ref, far_ref, far_near_ref, in_ref, out_ref,
):
    shares, share = both_ref.shape[0], both_ref.shape[1] // 2
    pieces = out_ref.shape[0] // share
    owner, core = relative(0), lax.axis_index("core")
    far_place = shares + core * pieces

    def chunks(ref, place, count):
        return jnp.concatenate([ref[place + k] for k in range(count)], axis=0)

    def quarters(refs, places):
        return [chunks(ref, place, pieces) for ref, place in zip(refs, places)]

    def products(left, right, to_ref):
        width = 384
        for at in range(0, to_ref.shape[1], width):
            part = dot(left, right[at : at + width], ((1,), (1,))) * factor
            to_ref[:, at : at + width] = part.astype(BF16)

    features = (own_features_ref, near_features_ref, far_features_ref, far_near_features_ref)
    others = (near_ref, far_ref, far_near_ref)
    acts = jnp.concatenate(quarters(features, (shares, shares, far_place, shares)), axis=1)
    own_grads = jnp.concatenate([both_ref[k, share:] for k in range(shares)], axis=0)
    grads = jnp.concatenate([own_grads] + [chunks(ref, 0, shares) for ref in others], axis=1)
    products(acts, grads, in_ref)
    own_hidden = jnp.concatenate([both_ref[owner * pieces + j, :share] for j in range(pieces)], axis=0)
    hidden = jnp.concatenate([own_hidden] + quarters(others, (shares, far_place, shares)), axis=1)
    cots = jnp.concatenate([chunks(ref, 0, shares) for ref in features], axis=1)
    products(hidden, cots, out_ref)


def call(kernel, name, outs, scratch, sems, args, in_hbm, flops, vmem, out_hbm=()):
    n_bytes = sum(a.size * a.dtype.itemsize for a in args)
    return pl.pallas_call(
        kernel,
        out_shape=outs,
        in_specs=[pl.BlockSpec(memory_space=pltpu.HBM) if i in in_hbm else VMEM for i in range(len(args))],
        out_specs=tuple(pl.BlockSpec(memory_space=pltpu.HBM) if i in out_hbm else VMEM for i in range(len(outs))),
        scratch_shapes=[pltpu.VMEM(*s) for s in scratch] + [pltpu.SemaphoreType.DMA(s) for s in sems],
        compiler_params=pltpu.CompilerParams(vmem_limit_bytes=vmem * 2**20),
        cost_estimate=pl.CostEstimate(flops=flops, bytes_accessed=n_bytes, transcendentals=0),
        name=name,
    )(*args)


def exchange(near, far):
    swap = [(0, 1), (1, 0)]
    far = lax.ppermute(far, "xh", swap)
    near = lax.ppermute(near, "core", swap)
    (far_near,) = call(
        forward, "forward", (jax.ShapeDtypeStruct(near.shape, BF16),), [], [(2,)], (far, near), (1,), 0, 32
    )
    return near, far, lax.ppermute(far_near, "core", swap)


def body(activations, weight_in, weight_out, cotangent):
    own, tokens = activations.shape
    feats, units = weight_in.shape
    n_gx, n_gy, n_dev = (lax.axis_size(a) for a in (GX, "gy", DEV))
    share = units // n_gy
    pair_rows = (2 * own, tokens)
    products = 4 * feats * units * tokens

    pair = jnp.concatenate([activations, cotangent], axis=0)
    block = lax.all_gather(pair, "z", axis=0, tiled=False)
    block = lax.all_gather(block, "xl", axis=0, tiled=True)
    weight = (weight_in.shape, BF16)
    rows = ((feats, tokens), F32)
    near_shape = jax.ShapeDtypeStruct((n_gy + n_gy // n_dev, share, tokens), BF16)
    far_shape = jax.ShapeDtypeStruct((n_gy + n_gy // 2, share, tokens), BF16)
    parts, own_features, near, far = call(
        unit_terms,
        "unit_terms",
        (jax.ShapeDtypeStruct((n_gy, 2 * share, tokens), BF16), near_shape, near_shape, far_shape),
        [((n_gx, *pair_rows), BF16), ((n_gy, 2 * share, tokens), BF16), ((2 * n_gy, feats // n_gy, tokens), BF16), weight, weight, rows, rows, (pair_rows, F32)],
        [(3 + n_gy // 2,), (6,)],
        (block, weight_in, weight_out),
        (0, 1, 2),
        products,
        62,
        (0, 1, 2, 3),
    )
    near_features, far_features, far_near_features = exchange(near, far)
    parts = lax.all_to_all(parts, "gy", 0, 0, tiled=True)
    (both,) = call(
        activate,
        "activate",
        (jax.ShapeDtypeStruct(parts.shape, BF16),),
        [],
        [],
        (parts, near_features, far_features),
        (1, 2),
        0,
        32,
    )
    both = lax.all_to_all(both, "gy", 0, 0, tiled=True)

    sums, near, far = call(
        feature_terms,
        "feature_terms",
        (jax.ShapeDtypeStruct((n_gx, *pair_rows), BF16), near_shape, far_shape),
        [((n_gy, 2 * share, tokens), BF16), ((n_gx, *pair_rows), BF16), weight, weight, rows, rows, (pair_rows, F32)],
        [(11,)],
        (both, weight_in, weight_out, far_near_features),
        (0, 1, 2, 3),
        products,
        62,
        (0, 1, 2),
    )
    near, far, far_near = exchange(near, far)
    sums = lax.all_to_all(sums, GX, 0, 0, tiled=True)
    sums = jnp.sum(sums.astype(F32), axis=0).astype(BF16)

    grads = call(
        functools.partial(weight_grads, 1.0 / math.sqrt(n_dev * tokens)),
        "weight_grads",
        (
            jax.ShapeDtypeStruct((feats // n_dev, units), BF16),
            jax.ShapeDtypeStruct((units // n_dev, feats), BF16),
        ),
        [],
        [],
        (own_features, near_features, far_features, far_near_features, both, near, far, far_near),
        (),
        products,
        32,
    )
    return (sums[:own], sums[own:], *grads)


def solution(mesh):
    shape = mesh.devices.shape
    fine = Mesh(
        mesh.devices.reshape(2, shape[0] // 2, shape[1], 2, shape[2] // 2),
        ("xl", "z", "gy", "xh", "core"),
    )
    return jax.shard_map(
        body,
        mesh=fine,
        in_specs=(P(("gy", *GX), DEV), P("gy", GX), P(GX, "gy"), P(("gy", *GX), DEV)),
        out_specs=(P(("gy", *GX), DEV), P(("gy", *GX), DEV), P(("gy", *DEV), GX), P((*GX, *DEV), "gy")),
        check_vma=False,
    )
```

```python
import functools
import math

import jax
import jax.numpy as jnp
from jax import lax
from jax.experimental import pallas as pl
from jax.experimental.pallas import tpu as pltpu
from jax.sharding import Mesh, PartitionSpec as P

F32 = jnp.float32
BF16 = jnp.bfloat16
GX = ("xl", "z")
DEV = ("xh", "core")
VMEM = pl.BlockSpec(memory_space=pltpu.VMEM)


def silu_slope(pre):
    sig = jax.nn.sigmoid(pre)
    return sig * (1.0 + pre * (1.0 - sig))


def dot(left, right, contract):
    return lax.dot_general(left, right, (contract, ((), ())), preferred_element_type=F32)


def turned(right):
    return right.astype(F32).T.astype(BF16)


def columns_dot(left, columns_ref, to_ref):
    width = 384
    for at in range(0, columns_ref.shape[1], width):
        to_ref[at : at + width] = dot(left, columns_ref[:, at : at + width], ((1,), (0,))).T


def unit_terms(
    block_hbm, in_hbm, out_hbm, parts_hbm, own_hbm, near_hbm, far_hbm,
    block_ref, parts_ref, features_ref, in_ref, out_ref, acts_ref, cots_ref, pair_ref, sems, feature_sems,
):
    load = pltpu.make_async_copy(block_hbm, block_ref, sems.at[0])
    load_in = pltpu.make_async_copy(in_hbm, in_ref, sems.at[1])
    load_out = pltpu.make_async_copy(out_hbm, out_ref, sems.at[2])
    load.start()
    load_in.start()
    own = block_ref.shape[1] // 2
    load.wait()
    load_out.start()
    for g in range(block_ref.shape[0]):
        pair_ref[...] = block_ref[g].astype(F32)
        acts_ref[g * own : (g + 1) * own] = pair_ref[:own]
        cots_ref[g * own : (g + 1) * own] = pair_ref[own:]
    cots, acts = cots_ref[...].astype(BF16), turned(acts_ref[...])
    pieces = features_ref.shape[0] // 2
    rows = features_ref.shape[1]
    for k in range(pieces):
        features_ref[k] = cots_ref[k * rows : (k + 1) * rows].astype(BF16)
        features_ref[pieces + k] = acts_ref[k * rows : (k + 1) * rows].astype(BF16)
    quarter, half = near_hbm.shape[0] - pieces, far_hbm.shape[0] - pieces
    stores = []
    for i, (target, start, count) in enumerate(
        [
            (near_hbm, relative(1) * quarter, quarter),
            (far_hbm, (1 - lax.axis_index("xh")) * half, half),
            (own_hbm, relative(0) * quarter, quarter),
        ]
    ):
        stores.append(
            pltpu.make_async_copy(features_ref.at[pl.ds(0, pieces)], target.at[pl.ds(0, pieces)], feature_sems.at[2 * i])
        )
        stores.append(
            pltpu.make_async_copy(
                features_ref.at[pl.ds(pieces + start, count)], target.at[pl.ds(pieces, count)], feature_sems.at[2 * i + 1]
            )
        )
    pre_ref = acts_ref
    load_in.wait()
    for store in stores:
        store.start()
    columns_dot(acts, in_ref, pre_ref)
    shares, share = parts_ref.shape[0], parts_ref.shape[1] // 2
    for k in range(shares):
        parts_ref[k, :share] = pre_ref[k * share : (k + 1) * share].astype(BF16)
    load_out.wait()
    each = 2
    for k in range(0, shares, each):
        grad = dot(out_ref[k * share : (k + each) * share], cots, ((1,), (0,))).astype(BF16)
        for j in range(each):
            parts_ref[k + j, share:] = grad[j * share : (j + 1) * share]
        part = pl.ds(k, each)
        stores.append(pltpu.make_async_copy(parts_ref.at[part], parts_hbm.at[part], sems.at[3 + k // each]))
        stores[-1].start()
    for store in stores:
        store.wait()


def activate(parts_ref, far_hbm, copies_ref):
    shares, share = parts_ref.shape[0], parts_ref.shape[1] // 2
    total = parts_ref[0].astype(F32)
    for k in range(1, shares):
        total = total + parts_ref[k].astype(F32)
    pre, grad_hidden = total[:share], total[share:]
    hidden = jax.nn.silu(pre).astype(BF16)
    grad_pre = (grad_hidden * silu_slope(pre)).astype(BF16)
    for k in range(shares):
        copies_ref[k, :share] = hidden
        copies_ref[k, share:] = grad_pre


def feature_terms(
    both_hbm, in_hbm, out_hbm, after_hbm, sums_hbm, near_hbm, far_hbm,
    both_ref, sums_ref, in_ref, out_ref, out_rows_ref, in_rows_ref, pair_ref, sems,
):
    shares, share = both_ref.shape[0], both_ref.shape[1] // 2
    load = pltpu.make_async_copy(both_hbm, both_ref, sems.at[0])
    load_in = pltpu.make_async_copy(in_hbm, in_ref, sems.at[10])
    load_out = pltpu.make_async_copy(out_hbm, out_ref, sems.at[1])
    load.start()
    load_in.start()
    quarter, half = near_hbm.shape[0] - shares, far_hbm.shape[0] - shares
    load.wait()
    stores = [
        pltpu.make_async_copy(source, target, sems.at[2 + i])
        for i, (source, target) in enumerate(
            [
                (both_ref.at[:, pl.ds(share, share)], near_hbm.at[pl.ds(0, shares)]),
                (both_ref.at[pl.ds(relative(1) * quarter, quarter), pl.ds(0, share)], near_hbm.at[pl.ds(shares, quarter)]),
                (both_ref.at[:, pl.ds(share, share)], far_hbm.at[pl.ds(0, shares)]),
                (both_ref.at[pl.ds((1 - lax.axis_index("xh")) * half, half), pl.ds(0, share)], far_hbm.at[pl.ds(shares, half)]),
            ]
        )
    ]
    load_out.start()
    for store in stores:
        store.start()
    grad = jnp.concatenate([both_ref[k, share:] for k in range(shares)], axis=0)
    load_in.wait()
    in_rows_ref[...] = dot(in_ref[...], grad, ((1,), (0,)))
    hidden = turned(jnp.concatenate([both_ref[k, :share] for k in range(shares)], axis=0))
    load_out.wait()
    columns_dot(hidden, out_ref, out_rows_ref)
    members, own = sums_ref.shape[0], sums_ref.shape[1] // 2
    each = members // 4
    for c in range(4):
        for g in range(c * each, (c + 1) * each):
            pair_ref[:own] = out_rows_ref[g * own : (g + 1) * own]
            pair_ref[own:] = in_rows_ref[g * own : (g + 1) * own]
            sums_ref[g] = pair_ref[...].astype(BF16)
        span = pl.ds(c * each, each)
        stores.append(pltpu.make_async_copy(sums_ref.at[span], sums_hbm.at[span], sems.at[6 + c]))
        stores[-1].start()
    for store in stores:
        store.wait()


def relative(step):
    xh, core = lax.axis_index("xh"), lax.axis_index("core")
    return 2 * (1 - xh if step & 2 else xh) + (1 - core if step & 1 else core)


def forward(far_ref, after_hbm, out_ref, sems):
    pieces = far_ref.shape[0] - out_ref.shape[0]
    shares = out_ref.shape[0] - pieces
    other = shares + (1 - lax.axis_index("core")) * pieces
    copies = [
        pltpu.make_async_copy(far_ref.at[pl.ds(0, shares)], out_ref.at[pl.ds(0, shares)], sems.at[0]),
        pltpu.make_async_copy(far_ref.at[pl.ds(other, pieces)], out_ref.at[pl.ds(shares, pieces)], sems.at[1]),
    ]
    for copy in copies:
        copy.start()
    for copy in copies:
        copy.wait()


def weight_grads(
    factor, own_features_ref, near_features_ref, far_features_ref, far_near_features_ref,
    both_ref, near_ref, far_ref, far_near_ref, in_ref, out_ref,
):
    shares, share = both_ref.shape[0], both_ref.shape[1] // 2
    pieces = out_ref.shape[0] // share
    owner, core = relative(0), lax.axis_index("core")
    far_place = shares + core * pieces

    def chunks(ref, place, count):
        return jnp.concatenate([ref[place + k] for k in range(count)], axis=0)

    def quarters(refs, places):
        return [chunks(ref, place, pieces) for ref, place in zip(refs, places)]

    def products(left, right, to_ref):
        width = 384
        for at in range(0, to_ref.shape[1], width):
            part = dot(left, right[at : at + width], ((1,), (1,))) * factor
            to_ref[:, at : at + width] = part.astype(BF16)

    features = (own_features_ref, near_features_ref, far_features_ref, far_near_features_ref)
    others = (near_ref, far_ref, far_near_ref)
    acts = jnp.concatenate(quarters(features, (shares, shares, far_place, shares)), axis=1)
    own_grads = jnp.concatenate([both_ref[k, share:] for k in range(shares)], axis=0)
    grads = jnp.concatenate([own_grads] + [chunks(ref, 0, shares) for ref in others], axis=1)
    products(acts, grads, in_ref)
    own_hidden = jnp.concatenate([both_ref[owner * pieces + j, :share] for j in range(pieces)], axis=0)
    hidden = jnp.concatenate([own_hidden] + quarters(others, (shares, far_place, shares)), axis=1)
    cots = jnp.concatenate([chunks(ref, 0, shares) for ref in features], axis=1)
    products(hidden, cots, out_ref)


def call(kernel, name, outs, scratch, sems, args, in_hbm, flops, vmem, out_hbm=()):
    n_bytes = sum(a.size * a.dtype.itemsize for a in args)
    return pl.pallas_call(
        kernel,
        out_shape=outs,
        in_specs=[pl.BlockSpec(memory_space=pltpu.HBM) if i in in_hbm else VMEM for i in range(len(args))],
        out_specs=tuple(pl.BlockSpec(memory_space=pltpu.HBM) if i in out_hbm else VMEM for i in range(len(outs))),
        scratch_shapes=[pltpu.VMEM(*s) for s in scratch] + [pltpu.SemaphoreType.DMA(s) for s in sems],
        compiler_params=pltpu.CompilerParams(vmem_limit_bytes=vmem * 2**20),
        cost_estimate=pl.CostEstimate(flops=flops, bytes_accessed=n_bytes, transcendentals=0),
        name=name,
    )(*args)


def exchange(near, far):
    swap = [(0, 1), (1, 0)]
    far = lax.ppermute(far, "xh", swap)
    near = lax.ppermute(near, "core", swap)
    (far_near,) = call(
        forward, "forward", (jax.ShapeDtypeStruct(near.shape, BF16),), [], [(2,)], (far, near), (1,), 0, 32
    )
    return near, far, lax.ppermute(far_near, "core", swap)


def body(activations, weight_in, weight_out, cotangent):
    own, tokens = activations.shape
    feats, units = weight_in.shape
    n_gx, n_gy, n_dev = (lax.axis_size(a) for a in (GX, "gy", DEV))
    share = units // n_gy
    pair_rows = (2 * own, tokens)
    products = 4 * feats * units * tokens

    pair = jnp.concatenate([activations, cotangent], axis=0)
    block = lax.all_gather(pair, "z", axis=0, tiled=False)
    block = lax.all_gather(block, "xl", axis=0, tiled=True)
    weight = (weight_in.shape, BF16)
    rows = ((feats, tokens), F32)
    near_shape = jax.ShapeDtypeStruct((n_gy + n_gy // n_dev, share, tokens), BF16)
    far_shape = jax.ShapeDtypeStruct((n_gy + n_gy // 2, share, tokens), BF16)
    parts, own_features, near, far = call(
        unit_terms,
        "unit_terms",
        (jax.ShapeDtypeStruct((n_gy, 2 * share, tokens), BF16), near_shape, near_shape, far_shape),
        [((n_gx, *pair_rows), BF16), ((n_gy, 2 * share, tokens), BF16), ((2 * n_gy, feats // n_gy, tokens), BF16), weight, weight, rows, rows, (pair_rows, F32)],
        [(3 + n_gy // 2,), (6,)],
        (block, weight_in, weight_out),
        (0, 1, 2),
        products,
        62,
        (0, 1, 2, 3),
    )
    near_features, far_features, far_near_features = exchange(near, far)
    parts = lax.all_to_all(parts, "gy", 0, 0, tiled=True)
    (both,) = call(
        activate,
        "activate",
        (jax.ShapeDtypeStruct(parts.shape, BF16),),
        [],
        [],
        (parts, far_features),
        (1,),
        0,
        32,
    )
    both = lax.all_to_all(both, "gy", 0, 0, tiled=True)

    sums, near, far = call(
        feature_terms,
        "feature_terms",
        (jax.ShapeDtypeStruct((n_gx, *pair_rows), BF16), near_shape, far_shape),
        [((n_gy, 2 * share, tokens), BF16), ((n_gx, *pair_rows), BF16), weight, weight, rows, rows, (pair_rows, F32)],
        [(11,)],
        (both, weight_in, weight_out, far_near_features),
        (0, 1, 2, 3),
        products,
        62,
        (0, 1, 2),
    )
    near, far, far_near = exchange(near, far)
    sums = lax.all_to_all(sums, GX, 0, 0, tiled=True)
    sums = jnp.sum(sums.astype(F32), axis=0).astype(BF16)

    grads = call(
        functools.partial(weight_grads, 1.0 / math.sqrt(n_dev * tokens)),
        "weight_grads",
        (
            jax.ShapeDtypeStruct((feats // n_dev, units), BF16),
            jax.ShapeDtypeStruct((units // n_dev, feats), BF16),
        ),
        [],
        [],
        (own_features, near_features, far_features, far_near_features, both, near, far, far_near),
        (),
        products,
        32,
    )
    return (sums[:own], sums[own:], *grads)


def solution(mesh):
    shape = mesh.devices.shape
    fine = Mesh(
        mesh.devices.reshape(2, shape[0] // 2, shape[1], 2, shape[2] // 2),
        ("xl", "z", "gy", "xh", "core"),
    )
    return jax.shard_map(
        body,
        mesh=fine,
        in_specs=(P(("gy", *GX), DEV), P("gy", GX), P(GX, "gy"), P(("gy", *GX), DEV)),
        out_specs=(P(("gy", *GX), DEV), P(("gy", *GX), DEV), P(("gy", *DEV), GX), P((*GX, *DEV), "gy")),
        check_vma=False,
    )
```
